32 devices in a mesh: seq: 8 (over y, x, core), fsdp: 4 (over z).
Axes of the slice: x: 2, y: 2, z: 4, core: 2. Of those that a mesh axis runs over, the one named last changes fastest.
Arguments:
- query: bfloat16 [4, 1280, 4096], P('fsdp', 'seq'), may hold values from -6 to 6
- key: bfloat16 [4, 1280, 4096], P('fsdp', 'seq'), may hold values from -6 to 6
- value: bfloat16 [4, 1280, 4096], P('fsdp', 'seq'), may hold values from -6 to 6
- stream: bfloat16 [4, 1280, 4096], P('fsdp', 'seq'), may hold values from -6 to 6
- targets: int32 [4, 1280], P('fsdp', 'seq'), may hold values from 0 to 3
- short_filter: float32 [7, 3, 2048], replicated, may hold values from -2 to 2
- med_filter: bfloat16 [128, 128], replicated, may hold values from -0.5 to 0.5
- out_weight: bfloat16 [2048, 2048], P('fsdp'), may hold values from -0.125 to 0.125
- head: float32 [4, 2048], replicated, may hold values from -0.09375 to 0.09375
Outputs:
- query_grad: bfloat16 [4, 1280, 4096], P('fsdp', 'seq')
- key_grad: bfloat16 [4, 1280, 4096], P('fsdp', 'seq')
- value_grad: bfloat16 [4, 1280, 4096], P('fsdp', 'seq')
- out_grad: float32 [2048, 2048], P('fsdp')
The draws below stay inside these ranges and needn't reach their ends.
All inputs are finite; a program needn't handle non-finite values.
Results may differ from the reference program's by a relative error of at most 0.022.
Values may be sent and summed in bfloat16 or wider, within the bound.
A program may use at most 192 MiB of HBM per device.

```python
import jax
import jax.numpy as jnp
from jax import lax

D = 4096
H = 2048
CPG = 16
GROUPS = 128
SHORT = 7
MED = 128
NUC = 4
GENOMES = 4
SEQ = 1280


def set_ends(array, key, low, top_value):
    longest = array.shape.index(max(array.shape))
    spots = []
    for shift in (0, 1):
        where = [jax.random.randint(jax.random.fold_in(key, axis), (), 0, length) for axis, length in enumerate(array.shape)]
        where[longest] = (where[longest] + shift) % array.shape[longest]
        spots.append(tuple(where))
    return array.at[spots[0]].set(low).at[spots[1]].set(top_value)


def spiked(drawn, key, source, target, blocks, factor):
    def block_of(axis_at):
        return (jnp.arange(drawn.shape[axis_at]) // (drawn.shape[axis_at] // blocks)).reshape((-1,) + (1,) * (drawn.ndim - 1 - axis_at))

    first = jax.random.permutation(key, blocks)[block_of(target)]
    other_side = (block_of(target) + blocks // 2) % blocks
    return jnp.where((block_of(source) == first) | (block_of(source) == other_side), factor * drawn, drawn)


def shard_levels(key, dims, pieces, least, top_value):
    def one(dim, shards_of):
        steps = jax.random.uniform(jax.random.fold_in(jax.random.fold_in(key, 6), dim), (shards_of,), jnp.float32, least / len(pieces), top_value / len(pieces))
        return jnp.repeat(jnp.exp(steps), dims[dim] // shards_of).reshape((-1,) + (1,) * (len(dims) - dim - 1))

    gain = one(*pieces[0])
    for cut in pieces[1:]:
        gain = gain * one(*cut)
    return gain


def normal_values(rng, extent, deviation, most, split=(), kind=jnp.bfloat16):
    loudness = shard_levels(rng, extent, split, -0.22, 0.18) if split else 1.0
    values = jax.random.normal(rng, extent, jnp.float32) * deviation * loudness
    return jnp.minimum(jnp.maximum(values, -most), most).astype(kind)


def gaussian_with(rng, shape, spread, bound, shards, heavy, kind=jnp.bfloat16):
    values = spread * jax.random.normal(rng, shape, jnp.float32)
    if shards:
        values = values * shard_levels(rng, shape, shards, -0.22, 0.18)
    return jnp.clip(spiked(values, jax.random.fold_in(rng, 3), *heavy), -bound, bound).astype(kind)


def setup_inputs(seed: int = 0) -> dict:
    streams_of = jax.random.split(jax.random.key(seed), 10)
    return {
        "query": gaussian_with(streams_of[0], (GENOMES, SEQ, D), 1.0, 6.0, ((0, 4), (1, 8)), (0, 2, 4, 2.0)),
        "key": normal_values(streams_of[1], (GENOMES, SEQ, D), 1.0, 6.0, ((0, 4), (1, 8))),
        "value": normal_values(streams_of[2], (GENOMES, SEQ, D), 1.0, 6.0, ((0, 4), (1, 8))),
        "stream": normal_values(streams_of[3], (GENOMES, SEQ, D), 1.0, 6.0, ((0, 4), (1, 8))),
        "targets": set_ends(jax.random.randint(streams_of[4], (GENOMES, SEQ), 0, NUC), jax.random.fold_in(streams_of[4], 1), 0, NUC - 1).astype(jnp.int32),
        "short_filter": normal_values(streams_of[5], (SHORT, 3, H), SHORT ** -0.5, 2.0, (), jnp.float32),
        "med_filter": normal_values(streams_of[6], (MED, GROUPS), MED ** -0.5, 0.5),
        "out_weight": normal_values(streams_of[7], (H, H), H ** -0.5, 0.125, ((0, 4),)),
        "head": normal_values(streams_of[8], (NUC, H), D ** -0.5, 0.09375, (), jnp.float32),
    }


loss_scale = 64.0


def causal_fft(signal, conv_taps):
    length = signal.shape[0]
    size_total = length + conv_taps.shape[0]
    spectrum = jnp.fft.rfft(signal, n=size_total, axis=0) * jnp.fft.rfft(conv_taps, n=size_total, axis=0)
    return jnp.fft.irfft(spectrum, n=size_total, axis=0)[:length]


def causal_short(signal, conv_taps):
    length = signal.shape[0]
    summed = conv_taps[0] * signal
    for offset in range(1, conv_taps.shape[0]):
        moved = jnp.pad(signal, ((offset, 0), (0, 0)))[:length]
        summed = summed + conv_taps[offset] * moved
    return summed


def orient(signal, flip_first, half_width):
    if flip_first:
        return jnp.concatenate([signal[::-1, :half_width], signal[:, half_width:]], axis=1)
    return jnp.concatenate([signal[:, :half_width], signal[::-1, half_width:]], axis=1)


def directed(signal, conv_taps, backward, use_fft):
    half_width = signal.shape[1] // 2
    both_taps = jnp.concatenate([conv_taps, conv_taps], axis=1)
    turned = orient(signal, backward, half_width)
    if use_fft:
        result = causal_fft(turned, both_taps)
    else:
        result = causal_short(turned, both_taps)
    return orient(result, backward, half_width)


def one_genome(query_g, key_g, value_g, stream_g, target_g, short_filter, med_filter, out_weight, head):
    half_width = D // 2
    length = query_g.shape[0]
    med_taps = jnp.repeat(med_filter.astype(jnp.float32), CPG, axis=1)
    feat_q = directed(query_g.astype(jnp.float32), short_filter[:, 0, :], False, False)
    feat_k = directed(key_g.astype(jnp.float32), short_filter[:, 1, :], False, False)
    feat_v = directed(value_g.astype(jnp.float32), short_filter[:, 2, :], False, False)
    gate = feat_q.astype(jnp.bfloat16)
    products = (feat_k * feat_v).astype(jnp.bfloat16)
    long_mix = directed(products.astype(jnp.float32), med_taps, False, True)
    gated = (gate.astype(jnp.float32) * long_mix).astype(jnp.bfloat16)
    gated_rows = jnp.concatenate([gated[:, :half_width], gated[:, half_width:]], axis=0)
    branch = jnp.dot(gated_rows, out_weight, preferred_element_type=jnp.float32)
    state = stream_g.astype(jnp.float32) + jnp.concatenate([branch[:length], branch[length:]], axis=1)
    flipped = head[::-1]
    logits = jnp.dot(state[:, :half_width], head.T, precision=lax.Precision.HIGHEST) + jnp.dot(
        state[:, half_width:], flipped.T, precision=lax.Precision.HIGHEST)
    exponent = jnp.exp(logits)
    softmax_out = exponent / jnp.sum(exponent, axis=1, keepdims=True)
    one_hot = (target_g[:, None] == jnp.arange(NUC, dtype=jnp.int32)[None, :]).astype(jnp.float32)
    logit_grad = loss_scale * (softmax_out - one_hot)
    state_grad = jnp.concatenate([
        jnp.dot(logit_grad, head, precision=lax.Precision.HIGHEST),
        jnp.dot(logit_grad, flipped, precision=lax.Precision.HIGHEST)], axis=1).astype(jnp.bfloat16)
    grad_rows = jnp.concatenate([state_grad[:, :half_width], state_grad[:, half_width:]], axis=0)
    gated_grad_rows = jnp.dot(grad_rows, out_weight.T, preferred_element_type=jnp.float32)
    gated_grad = jnp.concatenate([gated_grad_rows[:length], gated_grad_rows[length:]], axis=1)
    gate_grad = gated_grad * long_mix
    mix_grad = (gated_grad * gate.astype(jnp.float32)).astype(jnp.bfloat16)
    products_grad = directed(mix_grad.astype(jnp.float32), med_taps, True, True)
    key_feat_grad = products_grad * feat_v
    value_feat_grad = products_grad * feat_k
    query_out = directed(gate_grad, short_filter[:, 0, :], True, False).astype(jnp.bfloat16)
    key_out = directed(key_feat_grad, short_filter[:, 1, :], True, False).astype(jnp.bfloat16)
    value_out = directed(value_feat_grad, short_filter[:, 2, :], True, False).astype(jnp.bfloat16)
    weight_term = jnp.dot(gated_rows.T, grad_rows, preferred_element_type=jnp.float32)
    return query_out, key_out, value_out, weight_term


def reference(query, key, value, stream, targets, short_filter, med_filter, out_weight, head):
    def scan_step(carry, inputs):
        query_g, key_g, value_g, stream_g, target_g = inputs
        query_out, key_out, value_out, weight_term = one_genome(
            query_g, key_g, value_g, stream_g, target_g, short_filter, med_filter, out_weight, head)
        return carry + weight_term, (query_out, key_out, value_out)

    initial = jnp.zeros((D // 2, D // 2), jnp.float32)
    summed, grads = lax.scan(scan_step, initial, (query, key, value, stream, targets))
    return grads[0], grads[1], grads[2], summed / loss_scale
```

```python
import jax
import jax.numpy as jnp
from jax import lax
from jax.experimental import pallas as pl
from jax.experimental.pallas import tpu as pltpu
from jax.sharding import PartitionSpec as P

loss_scale = 64.0
LANES = 256
EDGE = 8
BLOCK = 128
VMEM_LIMIT = 48 * 1024 * 1024


def split_bf16(x):
    high = x.astype(jnp.bfloat16)
    low = (x - high.astype(jnp.float32)).astype(jnp.bfloat16)
    return high, low


def mm(a, b, ca=1, cb=0):
    return lax.dot_general(a, b, (((ca,), (cb,)), ((), ())), preferred_element_type=jnp.float32)


def banded(x_ref, base_ref, out_ref, tail_first):
    per_group = LANES // base_ref.shape[1]
    rows = out_ref.shape[0]
    rest = rows - BLOCK
    span = BLOCK + rest
    big_in, small_in = (rest, 0) if tail_first else (0, BLOCK)
    big_out, small_out = (rest, 0) if tail_first else (0, BLOCK)
    lane = lax.broadcasted_iota(jnp.int32, (1, BLOCK), 1) // per_group
    for part in range(LANES // BLOCK):
        cols = slice(part * BLOCK, (part + 1) * BLOCK)
        x_big = x_ref[big_in : big_in + 2 * BLOCK, cols]
        x_small = x_ref[small_in : small_in + span, cols]
        big = small = None
        for index in range(BLOCK // per_group):
            g = part * (BLOCK // per_group) + index
            row = jnp.broadcast_to(base_ref[0, g : g + 1, :], (BLOCK, 2 * BLOCK))
            toeplitz = pltpu.roll(row, 0, 1, stride=1, stride_axis=0).astype(jnp.bfloat16)
            one_big = mm(toeplitz, x_big)
            one_small = mm(toeplitz[:rest, :span], x_small)
            if index == 0:
                big, small = one_big, one_small
            else:
                here = lane == index
                big = jnp.where(here, one_big, big)
                small = jnp.where(here, one_small, small)
        out_ref[big_out : big_out + BLOCK, cols] = big
        out_ref[small_out : small_out + rest, cols] = small


def featured_kernel(q_ref, k_ref, v_ref, rim_ref, taps_ref, gate_ref, fk_ref, fv_ref, prod_ref, raw):
    count = q_ref.shape[0]
    taps = taps_ref.shape[0]
    wide = count + EDGE
    blank = jnp.zeros((EDGE, LANES), jnp.float32)

    def run(reverse):
        feats = []
        for m, ref in enumerate((q_ref, k_ref, v_ref)):
            rim = rim_ref[m].astype(jnp.float32)
            raw[m, :EDGE] = rim[:EDGE]
            raw[m, EDGE : EDGE + count] = ref[...].astype(jnp.float32)
            raw[m, EDGE + count :] = rim[EDGE:]
            total = None
            for j in range(taps):
                start = j if reverse else EDGE - j
                term = taps_ref[j, m : m + 1, :] * raw[m, start : start + wide, :]
                total = term if total is None else total + term
            feats.append(jnp.concatenate([blank, total] if reverse else [total, blank], axis=0))
        gate_ref[0] = feats[0].astype(jnp.bfloat16)
        fk_ref[0] = feats[1]
        fv_ref[0] = feats[2]
        prod_ref[0] = (feats[1] * feats[2]).astype(jnp.bfloat16)

    for half in (0, 1):
        pl.when(pl.program_id(0) == half)(lambda half=half: run(half == 1))


def mix_kernel(prod_ref, low_ref, high_ref, gate_ref, stream_ref, base_ref, m_ref, head_ref, target_ref,
               mix_ref, lg_ref, a_ref, x, gated_s, logits):
    half, tile = pl.program_id(0), pl.program_id(1)
    tiles = pl.num_programs(1)
    count = stream_ref.shape[0]
    rows = prod_ref.shape[1]

    @pl.when((half == 0) & (tile == 0))
    def _():
        logits[...] = jnp.zeros_like(logits)

    def run(reverse):
        if reverse:
            x[:rows] = prod_ref[0]
            x[rows:] = high_ref[...]
        else:
            x[:BLOCK] = low_ref[...]
            x[BLOCK:] = prod_ref[0]
        banded(x, base_ref, mix_ref.at[0], reverse)
        first = rows - count if reverse else 0
        mix = mix_ref[0, first : first + count, :]
        gated = (gate_ref[0, first : first + count, :].astype(jnp.float32) * mix).astype(jnp.bfloat16)
        gated_s[half * tiles + tile] = gated
        m_high, m_low = split_bf16(m_ref[0])
        h_high, h_low = split_bf16(head_ref[0])
        stream = stream_ref[...]
        logits[...] += (mm(gated, m_high, 1, 1) + mm(gated, m_low, 1, 1)) + (
            mm(stream, h_high, 1, 1) + mm(stream, h_low, 1, 1))

    for side in (0, 1):
        pl.when(half == side)(lambda side=side: run(side == 1))

    @pl.when((half == 1) & (tile == tiles - 1))
    def _():
        lane = lax.broadcasted_iota(jnp.int32, logits.shape, 1)
        exponent = jnp.where(lane < 4, jnp.exp(logits[...]), 0.0)
        softmax_out = exponent / jnp.sum(exponent, axis=1, keepdims=True)
        grad = loss_scale * (softmax_out - jnp.where(lane == target_ref[...], 1.0, 0.0))
        lg_ref[...] = grad
        g_high, g_low = split_bf16(grad)

        @pl.loop(0, gated_s.shape[0])
        def _(i):
            block = gated_s[i]
            a_ref[i] = mm(g_high, block, 0, 0) + mm(g_low, block, 0, 0)


def grad_kernel(gate_ref, glow_ref, ghigh_ref, lg_ref, llow_ref, lhigh_ref, m_ref, mix_ref, fk_ref, fv_ref, base_ref,
                taps_ref, qo_ref, ko_ref, vo_ref, x, grads, pg, feat):
    count = lg_ref.shape[0]
    rows = gate_ref.shape[1]
    taps = taps_ref.shape[0]
    far = glow_ref.shape[0]

    def run(reverse):
        m_high, m_low = split_bf16(m_ref[0])
        if reverse:
            pieces = ((0, far, llow_ref[...], glow_ref[...]), (far, count, lg_ref[...], gate_ref[0, rows - count :, :]))
        else:
            pieces = ((0, count, lg_ref[...], gate_ref[0, :count, :]), (count, far, lhigh_ref[...], ghigh_ref[...]))
        for start, size, lg, gate in pieces:
            g_high, g_low = split_bf16(lg)
            part = mm(g_high, m_high) + (mm(g_high, m_low) + mm(g_low, m_high))
            grads[start : start + size] = part
            x[start : start + size] = (part * gate.astype(jnp.float32)).astype(jnp.bfloat16)
        banded(x, base_ref, pg, reverse)
        own = count + far - rows if reverse else 0
        feat[0] = grads[own : own + rows, :] * mix_ref[0]
        feat[1] = pg[...] * fv_ref[0]
        feat[2] = pg[...] * fk_ref[0]
        for m, out in enumerate((qo_ref, ko_ref, vo_ref)):
            total = None
            for j in range(taps):
                start = rows - count - j if reverse else j
                term = taps_ref[j, m : m + 1, :] * feat[m, start : start + count, :]
                total = term if total is None else total + term
            out[...] = total.astype(jnp.bfloat16)

    for side in (0, 1):
        pl.when(pl.program_id(0) == side)(lambda side=side: run(side == 1))


def per_device(query, key, value, stream, targets, short_filter, med_filter, out_weight, head):
    genomes, count, width = query.shape
    assert genomes == 1
    half = width // 2
    taps = short_filter.shape[0]
    tiles = half // LANES
    rows = count + 2 * EDGE
    far = count - 2 * EDGE
    groups = med_filter.shape[1]
    tile_groups = groups // tiles
    assert med_filter.shape[0] == BLOCK and BLOCK < rows <= 2 * BLOCK and rows + BLOCK == count + far and taps <= EDGE
    f32, bf16 = jnp.float32, jnp.bfloat16
    query, key, value, stream = (a.reshape(count, width) for a in (query, key, value, stream))
    seqs = lax.axis_size("seq")
    up = [(i, i + 1) for i in range(seqs - 1)]
    down = [(i + 1, i) for i in range(seqs - 1)]

    def to_right(a):
        return lax.ppermute(a, "seq", up)

    def to_left(a):
        return lax.ppermute(a, "seq", down)

    rim = jnp.concatenate([
        to_right(jnp.stack([a[count - EDGE :] for a in (query, key, value)])),
        to_left(jnp.stack([a[:EDGE] for a in (query, key, value)])),
    ], axis=1)

    head16 = jnp.pad(head, ((0, 12), (0, 0)))
    head2 = jnp.stack([head16, jnp.pad(head[::-1], ((0, 12), (0, 0)))])
    w_high = out_weight
    m_part = jnp.dot(head, w_high.T.astype(f32), precision=lax.Precision.HIGHEST)
    m_full = lax.all_gather(m_part, "fsdp", axis=1, tiled=True)
    m2 = jnp.stack([jnp.pad(m_full, ((0, 12), (0, 0))), jnp.pad(m_full[::-1], ((0, 12), (0, 0)))])

    table = med_filter.T.astype(f32)
    base = jnp.stack([
        jnp.pad(table[:, ::-1], ((0, 0), (1, BLOCK - 1))),
        jnp.pad(table, ((0, 0), (0, BLOCK))),
    ])

    sds = jax.ShapeDtypeStruct
    params = pltpu.CompilerParams(vmem_limit_bytes=VMEM_LIMIT, dimension_semantics=("arbitrary", "arbitrary"))
    whole = pl.BlockSpec((count, LANES), lambda h, t: (0, h * tiles + t))
    framed = pl.BlockSpec((1, rows, LANES), lambda h, t: (h, 0, t))
    taps_spec = pl.BlockSpec((taps, 3, LANES), lambda h, t: (0, 0, t))
    small = pl.BlockSpec((1, 16, LANES), lambda h, t: (h, 0, t))

    def fixed(*shape):
        return pl.BlockSpec(shape, lambda h, t: (0,) * len(shape))

    def low_side(size):
        return pl.BlockSpec((size, LANES), lambda h, t: (0, t * (1 - h) + (tiles - 1) * h))

    def high_side(size):
        return pl.BlockSpec((size, LANES), lambda h, t: (0, t * h))

    gate, feat_k, feat_v, prod = pl.pallas_call(
        featured_kernel,
        grid=(2, tiles),
        in_specs=[whole, whole, whole, pl.BlockSpec((3, 2 * EDGE, LANES), lambda h, t: (0, 0, h * tiles + t)), taps_spec],
        out_specs=[framed] * 4,
        out_shape=[sds((2, rows, half), bf16), sds((2, rows, half), f32), sds((2, rows, half), f32),
                   sds((2, rows, half), bf16)],
        scratch_shapes=[pltpu.VMEM((3, count + 2 * EDGE, LANES), f32)],
        compiler_params=params,
        cost_estimate=pl.CostEstimate(flops=14 * 3 * count * width, bytes_accessed=20 * count * width, transcendentals=0),
        name="featured",
    )(query, key, value, rim, short_filter)

    prod_low = to_right(prod[0, count - BLOCK : count])
    prod_high = to_left(prod[1, rows - count : rows - count + BLOCK])
    gate_high = to_left(gate[0, :far])
    gate_low = to_right(gate[1, rows - far :])

    mix, lg, a_part = pl.pallas_call(
        mix_kernel,
        grid=(2, tiles),
        in_specs=[framed, low_side(BLOCK), high_side(BLOCK), framed, whole,
                  pl.BlockSpec((1, tile_groups, 2 * BLOCK), lambda h, t: (h, t, 0)),
                  small, small, fixed(count, 1)],
        out_specs=[framed, fixed(count, 16), fixed(2 * tiles, 16, LANES)],
        out_shape=[sds((2, rows, half), f32), sds((count, 16), f32), sds((2 * tiles, 16, LANES), f32)],
        scratch_shapes=[pltpu.VMEM((rows + BLOCK, LANES), bf16), pltpu.VMEM((2 * tiles, count, LANES), bf16),
                        pltpu.VMEM((count, 16), f32)],
        compiler_params=params,
        cost_estimate=pl.CostEstimate(flops=512 * count * width * 8, bytes_accessed=12 * count * width, transcendentals=0),
        name="long_mix",
    )(prod, prod_low, prod_high, gate, stream, base, m2, head2, targets.reshape(count, 1))

    lg_high = to_left(lg[:far])
    lg_low = to_right(lg[count - far :])

    a_rows = a_part[:, :4].reshape(2, tiles, 4, LANES).transpose(0, 2, 1, 3).reshape(2, 4, half)
    a_sum = lax.psum(a_rows[0] + a_rows[1, ::-1], ("fsdp", "seq"))

    query_grad, key_grad, value_grad = pl.pallas_call(
        grad_kernel,
        grid=(2, tiles),
        in_specs=[framed, low_side_far(far, tiles), high_side_far(far, tiles), fixed(count, 16), fixed(far, 16),
                  fixed(far, 16), small, framed, framed, framed,
                  pl.BlockSpec((1, tile_groups, 2 * BLOCK), lambda h, t: (1 - h, t, 0)), taps_spec],
        out_specs=[whole] * 3,
        out_shape=[sds((count, width), bf16)] * 3,
        scratch_shapes=[pltpu.VMEM((count + far, LANES), bf16), pltpu.VMEM((count + far, LANES), f32),
                        pltpu.VMEM((rows, LANES), f32), pltpu.VMEM((3, rows, LANES), f32)],
        compiler_params=params,
        cost_estimate=pl.CostEstimate(flops=512 * count * width * 8, bytes_accessed=24 * count * width, transcendentals=0),
        name="input_grads",
    )(gate, gate_low, gate_high, lg, lg_low, lg_high, m2, mix, feat_k, feat_v, base, short_filter)

    own = out_weight.shape[0]
    mine = lax.dynamic_slice_in_dim(a_sum, lax.axis_index("fsdp") * own, own, axis=1) / loss_scale
    out_grad = sum(mine[v][:, None] * head[v][None, :] for v in range(head.shape[0]))
    return (query_grad[None], key_grad[None], value_grad[None], out_grad)


def low_side_far(size, tiles):
    return pl.BlockSpec((size, LANES), lambda h, t: (0, t * h))


def high_side_far(size, tiles):
    return pl.BlockSpec((size, LANES), lambda h, t: (0, t * (1 - h) + (tiles - 1) * h))


def solution(mesh):
    rows = P("fsdp", "seq", None)
    return jax.shard_map(
        per_device,
        mesh=mesh,
        in_specs=(rows, rows, rows, rows, P("fsdp", "seq"), P(), P(), P("fsdp", None), P()),
        out_specs=(rows, rows, rows, P("fsdp", None)),
        check_vma=False,
    )
```

```python
import functools

import jax
import jax.numpy as jnp
from jax import lax
from jax.experimental import pallas as pl
from jax.experimental.pallas import tpu as pltpu
from jax.sharding import PartitionSpec as P

loss_scale = 64.0
LANES = 256
PART = 128
EDGE = 8
RIM = 16
ROWS = 96
NUC = 4
MESH = pl.DeviceIdType.MESH
VMEM_LIMIT = 58 * 1024 * 1024
f32, bf16 = jnp.float32, jnp.bfloat16


def split_bf16(x):
    high = x.astype(bf16)
    low = (x - high.astype(f32)).astype(bf16)
    return high, low


def mm(a, b, ca=1, cb=0):
    return lax.dot_general(a, b, (((ca,), (cb,)), ((), ())), preferred_element_type=f32)


def short_conv(taps, x, first, step, size):
    near = far = None
    for j in range(4):
        moved = x(first + step * j, size)
        term = taps[j] * moved
        near = term if near is None else near + term
        if j + 4 < len(taps):
            term = taps[j + 4] * moved
            far = term if far is None else far + term
    return near, far


def placed(size, reverse, source):
    r = lax.broadcasted_iota(jnp.int32, (size, 16), 0)
    c = lax.broadcasted_iota(jnp.int32, (size, 16), 1)
    v = r % 16
    row = (3 - v if reverse else v) + source(r // 16)
    return jnp.where((v < 4) & (c == row), 1.0, 0.0).astype(bf16)


def block_kernel(
    sizes, q_hbm, k_hbm, v_hbm, stream_hbm, target_ref, taps_ref, med_ref, w_hbm, head_ref,
    qo_ref, ko_ref, vo_ref, a_ref,
    q_ref, k_ref, v_ref, stream_ref, w_ref, done,
    rim_low, rim_high, raw, gate, prod, prod_low, prod_high, gate_low, gate_high, feat_k, feat_v, mix, toep,
    x, gated_s, logits, lg, lg_low, lg_high, head8, m_all, m_full, m_cat, n_cat, coef, grads, pg, feat, a_own, a_in,
    b_in, b_own,
    in_sems, out_sems, rim_ss, rim_rs, prod_ss, prod_rs, gate_ss, gate_rs, lg_ss, lg_rs, m_ss, m_rs, a_ss, a_rs,
    b_ss, b_rs,
):
    seqs, shards = sizes
    s, f = lax.axis_index("seq"), lax.axis_index("fsdp")
    count, width = q_ref.shape
    half = width // 2
    tiles = half // LANES
    rows = gate.shape[1]
    far = gate_low.shape[0]
    taps_n = taps_ref.shape[1]
    own = w_ref.shape[0]
    has_left, has_right = s > 0, s < seqs - 1
    loads = [
        pltpu.make_async_copy(src, dst, in_sems.at[i])
        for i, (src, dst) in enumerate(
            ((w_hbm, w_ref), (q_hbm, q_ref), (k_hbm, k_ref), (v_hbm, v_ref), (stream_hbm, stream_ref)))
    ]
    for load in loads:
        load.start()
    left, right = (s - 1, f), (s + 1, f)

    def seq_peer(d):
        return lax.rem(s + d, seqs)

    def shard_peer(d):
        return lax.rem(f + d, shards)

    barrier = pltpu.get_barrier_semaphore()
    for d in range(1, seqs):
        pl.semaphore_signal(barrier, inc=1, device_id=(seq_peer(d), f), device_id_type=MESH)
    for d in range(1, shards):
        pl.semaphore_signal(barrier, inc=1, device_id=(s, shard_peer(d)), device_id_type=MESH)
    pl.semaphore_wait(barrier, seqs + shards - 2)

    def send(src, dst, ss, rs, to):
        return pltpu.make_async_remote_copy(src_ref=src, dst_ref=dst, send_sem=ss, recv_sem=rs, device_id=to,
                                            device_id_type=MESH)

    def cols(t):
        return pl.ds(pl.multiple_of(t * LANES, LANES), LANES)

    def rim_copy(side, m):
        ref = (q_hbm, k_hbm, v_hbm)[m]
        if side == 0:
            return send(ref.at[count - RIM :], rim_low.at[m], rim_ss.at[side, m], rim_rs.at[side, m], right)
        return send(ref.at[:RIM], rim_high.at[m], rim_ss.at[side, m], rim_rs.at[side, m], left)

    def prod_copy(side, t):
        if side == 0:
            return send(prod.at[0, count - PART : count, cols(t)], prod_low.at[:, cols(t)], prod_ss.at[side, t],
                        prod_rs.at[side, t], right)
        return send(prod.at[1, rows - count : rows - count + PART, cols(t)], prod_high.at[:, cols(t)],
                    prod_ss.at[side, t], prod_rs.at[side, t], left)

    def gate_copy(side, t):
        if side == 0:
            return send(gate.at[1, rows - far :, cols(t)], gate_low.at[:, cols(t)], gate_ss.at[side, t],
                        gate_rs.at[side, t], right)
        return send(gate.at[0, :far, cols(t)], gate_high.at[:, cols(t)], gate_ss.at[side, t], gate_rs.at[side, t], left)

    def lg_copy(side):
        if side == 0:
            return send(lg.at[count - far :], lg_low, lg_ss.at[side], lg_rs.at[side], right)
        return send(lg.at[:far], lg_high, lg_ss.at[side], lg_rs.at[side], left)

    sends = (has_right, has_left)
    gets = (has_left, has_right)

    def start(side, copy):
        pl.when(sends[side])(lambda: copy.start())

    def sent(side, copy):
        pl.when(sends[side])(lambda: copy.wait_send())

    def arrived(side, copy):
        pl.when(gets[side])(lambda: copy.wait_recv())

    def clear(refs, absent):
        @pl.when(absent)
        def _():
            for ref in refs:
                ref[...] = jnp.zeros_like(ref)

    for side in (0, 1):
        for m in range(3):
            start(side, rim_copy(side, m))
    clear((rim_low, prod_low, gate_low, lg_low), s == 0)
    clear((rim_high, prod_high, gate_high, lg_high), s == seqs - 1)

    head8[...] = jnp.zeros_like(head8)
    head8[: head_ref.shape[0]] = head_ref[...]

    def stacked(value):
        high, low = split_bf16(value)
        return jnp.concatenate([high.astype(f32), low.astype(f32)], axis=0).astype(bf16)

    h_cat = stacked(head8[...])
    loads[0].wait()
    both = mm(h_cat, w_ref[...], 1, 1)
    m_all[f] = both[:8] + both[8:]

    def m_copy(d, slot):
        return send(m_all.at[f], m_all.at[slot], m_ss.at[d - 1], m_rs.at[slot], (s, shard_peer(d)))

    for d in range(1, shards):
        m_copy(d, f).start()

    med = med_ref[...]
    tap = lax.broadcasted_iota(jnp.int32, (PART, 2 * PART), 0)
    place = lax.broadcasted_iota(jnp.int32, (PART, 2 * PART), 1)
    for o, here in enumerate((place == PART - tap, place == tap)):
        grads[:PART, :] = mm(med, jnp.where(here, 1.0, 0.0).astype(bf16), 0, 0)

        @pl.loop(0, toep.shape[1])
        def _(i):
            base = grads[pl.ds(pl.multiple_of(i * 8, 8), 8), :]
            for g in range(8):
                row = jnp.broadcast_to(base[g : g + 1, :], (ROWS, 2 * PART))
                toep[o, i, g * ROWS : (g + 1) * ROWS, :] = pltpu.roll(row, 0, 1, stride=1, stride_axis=0).astype(bf16)

    def banded(o, t, x, out_ref, slot):
        span = ROWS + PART
        late = rows - ROWS
        lane = lax.rem(lax.broadcasted_iota(jnp.int32, (1, 2 * PART), 1), PART) // (PART // 8)
        for part in range(LANES // PART):
            here = slice(part * PART, (part + 1) * PART)
            two = jnp.concatenate([x[:span, here], x[late : late + span, here]], axis=1)
            every = mm(toep[o, t * (LANES // PART) + part, :, :span], two)
            got = every[:ROWS]
            for g in range(1, 8):
                got = jnp.where(lane == g, every[g * ROWS : (g + 1) * ROWS], got)
            out_ref[slot, :ROWS, here] = got[:, :PART]
            out_ref[slot, late:, here] = got[:, PART:]

    def low_half(i):
        return jnp.where(i == 1, 8, 0)

    for h in (0, 1):
        n_cat[h] = mm(placed(32, h == 1, low_half), h_cat).astype(bf16)

    for load in loads[1:]:
        load.wait()
    for side in (0, 1):
        for m in range(3):
            arrived(side, rim_copy(side, m))

    for h in (0, 1):
        blank = jnp.zeros((EDGE, LANES), f32)

        def featured(t, raw):
            there = pl.ds(pl.multiple_of(h * half + t * LANES, LANES), LANES)
            feats = []
            for m, ref in enumerate((q_ref, k_ref, v_ref)):
                raw[m, :RIM] = rim_low[m, :, there].astype(f32)
                raw[m, RIM : RIM + count] = ref[:, there].astype(f32)
                raw[m, RIM + count :] = rim_high[m, :, there].astype(f32)
                taps = [taps_ref[m, j : j + 1, cols(t)] for j in range(taps_n)]
                near, away = short_conv(taps, lambda a, n: raw[m, a : a + n, :], EDGE, 1 if h else -1, rows)
                if h:
                    value = jnp.concatenate([blank, near[: rows - EDGE] + away[4 : rows - 4]], axis=0)
                else:
                    value = jnp.concatenate([near[EDGE:] + away[4 : rows - 4], blank], axis=0)
                feats.append(value)
            gate[h, :, cols(t)] = feats[0].astype(bf16)
            feat_k[h, :, cols(t)] = feats[1]
            feat_v[h, :, cols(t)] = feats[2]
            prod[h, :, cols(t)] = (feats[1] * feats[2]).astype(bf16)

        @pl.loop(0, tiles // 2)
        def _(i):
            for u in (0, 1):
                featured(2 * i + u, raw.at[u])
            for u in (0, 1):
                start(h, prod_copy(h, 2 * i + u))
                start(1 - h, gate_copy(1 - h, 2 * i + u))

    for d in range(1, shards):
        m_copy(d, shard_peer(d)).wait_recv()
    for p in range(shards):
        m_full[:, p * own : (p + 1) * own] = m_all[p]
    both_m = stacked(m_full[...])
    for h in (0, 1):
        m_cat[h] = mm(placed(48, h == 1, low_half), both_m).astype(bf16)

    logits[...] = jnp.zeros_like(logits)
    for h in (0, 1):

        def mixed(t, x):
            if h:
                x[:rows] = prod[1, :, cols(t)]
                x[rows:] = prod_high[:, cols(t)]
            else:
                x[:PART] = prod_low[:, cols(t)]
                x[PART:] = prod[0, :, cols(t)]
            banded(h, t, x, mix, h * tiles + t)
            first = rows - count if h else 0
            gated = (gate[h, first : first + count, cols(t)].astype(f32)
                     * mix[h * tiles + t, first : first + count, :]).astype(bf16)
            gated_s[h * tiles + t] = gated
            stream = stream_ref[:, pl.ds(pl.multiple_of(h * half + t * LANES, LANES), LANES)]
            return mm(gated, m_cat[h, :32, cols(t)], 1, 1) + mm(stream, n_cat[h, :, cols(t)], 1, 1)

        @pl.loop(0, tiles // 2)
        def _(i):
            for u in (0, 1):
                arrived(h, prod_copy(h, 2 * i + u))
            one, two = (mixed(2 * i + u, x.at[u]) for u in (0, 1))
            logits[:, :32] += one + two

    sums = logits[...]
    sums = (sums + pltpu.roll(sums, PART - 16, 1))[:, :16]
    lane = lax.broadcasted_iota(jnp.int32, sums.shape, 1)
    hot = lax.broadcasted_iota(jnp.int32, (16, count), 0) == target_ref[...]
    hot = jnp.where(hot, 1.0, 0.0).astype(bf16)
    eye = lax.broadcasted_iota(jnp.int32, (16, 16), 0) == lax.broadcasted_iota(jnp.int32, (16, 16), 1)
    one_hot = mm(hot, jnp.where(eye, 1.0, 0.0).astype(bf16), 0, 0)
    exponent = jnp.where(lane < 4, jnp.exp(sums), 0.0)
    softmax_out = exponent / jnp.sum(exponent, axis=1, keepdims=True)
    grad = loss_scale * (softmax_out - one_hot)
    lg[...] = grad
    for side in (0, 1):
        start(side, lg_copy(side))

    g_high, g_low = split_bf16(grad)
    swap = (lax.broadcasted_iota(jnp.int32, (16, 16), 0) + lax.broadcasted_iota(jnp.int32, (16, 16), 1)) == 3
    swap = jnp.where(swap, 1.0, 0.0).astype(bf16)
    r_high, r_low = mm(g_high, swap).astype(bf16), mm(g_low, swap).astype(bf16)

    @pl.loop(0, tiles)
    def _(t):
        one, two = gated_s[t], gated_s[tiles + t]
        total = (mm(g_high, one, 0, 0) + mm(g_low, one, 0, 0)) + (mm(r_high, two, 0, 0) + mm(r_low, two, 0, 0))
        a_own[:, cols(t)] = total[:8]

    def a_copy(d, slot):
        p = shard_peer(d)
        return send(a_own.at[:, pl.ds(pl.multiple_of(p * own, 128), own)], a_in.at[slot], a_ss.at[d - 1],
                    a_rs.at[slot], (s, p))

    def b_copy(d, slot):
        return send(b_own, b_in.at[slot], b_ss.at[d - 1], b_rs.at[slot], (seq_peer(d), f))

    for d in range(1, shards):
        a_copy(d, f).start()

    spot = lax.broadcasted_iota(jnp.int32, (16, 48), 1)
    lane48 = lax.broadcasted_iota(jnp.int32, (16, 48), 0)
    to_high = jnp.where((spot == lane48) | (spot == lane48 + 16), 1.0, 0.0).astype(bf16)
    to_low = jnp.where(spot == lane48 + 32, 1.0, 0.0).astype(bf16)

    def spread(value):
        high, low = split_bf16(value)
        return (mm(high, to_high) + mm(low, to_low)).astype(bf16)

    local = spread(lg[...])
    coef[0, :count] = local
    coef[1, far:] = local
    for side in (0, 1):
        arrived(side, lg_copy(side))
    coef[0, count:] = spread(lg_high[...])
    coef[1, :far] = spread(lg_low[...])

    def out_copy(m, h, t):
        there = pl.ds(pl.multiple_of(h * half + t * LANES, LANES), LANES)
        return pltpu.make_async_copy(done.at[m, :, there], (qo_ref, ko_ref, vo_ref)[m].at[:, there],
                                     out_sems.at[m, h * tiles + t])

    for h in (0, 1):

        def backward(t, x, grads, pg, feat):
            part = mm(coef[h], m_cat[h, :, cols(t)])
            if h:
                factors = ((0, far, gate_low[:, cols(t)]), (far, count, gate[1, rows - count :, cols(t)]))
            else:
                factors = ((0, count, gate[0, :count, cols(t)]), (count, far, gate_high[:, cols(t)]))
            for at, size, factor in factors:
                x[at : at + size] = (part[at : at + size] * factor.astype(f32)).astype(bf16)
            mine = count + far - rows if h else 0
            feat[0] = part[mine : mine + rows, :] * mix[h * tiles + t]
            banded(1 - h, t, x, pg, 0)
            feat[1] = pg[0] * feat_v[h, :, cols(t)]
            feat[2] = pg[0] * feat_k[h, :, cols(t)]
            there = pl.ds(pl.multiple_of(h * half + t * LANES, LANES), LANES)
            for m in range(3):
                taps = [taps_ref[m, j : j + 1, cols(t)] for j in range(taps_n)]
                size = count + EDGE
                near, away = short_conv(taps, lambda a, n: feat[m, a : a + n, :], EDGE if h else 0, -1 if h else 1, size)
                near = near[EDGE:] if h else near[:count]
                done[m, :, there] = (near + away[4 : 4 + count]).astype(bf16)

        @pl.loop(0, tiles // 2)
        def _(i):
            for u in (0, 1):
                arrived(1 - h, gate_copy(1 - h, 2 * i + u))
            for u in (0, 1):
                backward(2 * i + u, x.at[u], grads, pg.at[u], feat.at[u])
            for u in (0, 1):
                for m in range(3):
                    out_copy(m, h, 2 * i + u).start()

        if h == 0:
            total = a_own[:, pl.ds(pl.multiple_of(f * own, 128), own)]
            for d in range(1, shards):
                a_copy(d, shard_peer(d)).wait_recv()
                total = total + a_in[shard_peer(d)]
            b_own[...] = total
            for d in range(1, seqs):
                b_copy(d, s).start()

    total = b_own[...]
    for d in range(1, seqs):
        b_copy(d, seq_peer(d)).wait_recv()
        total = total + b_in[seq_peer(d)]
    a_ref[...] = total * (1.0 / loss_scale)

    @pl.loop(0, tiles)
    def _(t):
        for h in (0, 1):
            for m in range(3):
                out_copy(m, h, t).wait()

    for side in (0, 1):
        for m in range(3):
            sent(side, rim_copy(side, m))
        sent(side, lg_copy(side))

        @pl.loop(0, tiles)
        def _(t):
            sent(side, prod_copy(side, t))
            sent(side, gate_copy(side, t))

    for d in range(1, shards):
        m_copy(d, f).wait_send()
        a_copy(d, f).wait_send()
    for d in range(1, seqs):
        b_copy(d, s).wait_send()


def finish_kernel(a_ref, head_ref, q_ref, k_ref, v_ref, qo_ref, ko_ref, vo_ref, out_ref, head8):
    @pl.when(pl.program_id(0) == 0)
    def _():
        head8[...] = jnp.zeros_like(head8)
        head8[: head_ref.shape[0]] = head_ref[...]

    for src, dst in ((q_ref, qo_ref), (k_ref, ko_ref), (v_ref, vo_ref)):
        dst[...] = src[...]
    a_high, a_low = split_bf16(a_ref[...])
    h_high, h_low = split_bf16(head8[...])
    out_ref[...] = mm(a_high, h_high, 0, 0) + (mm(a_high, h_low, 0, 0) + mm(a_low, h_high, 0, 0))


def per_device(sizes, query, key, value, stream, targets, short_filter, med_filter, out_weight, head):
    genomes, count, width = query.shape
    half = width // 2
    tiles = half // LANES
    rows = count + 2 * EDGE
    far = count - RIM
    own = out_weight.shape[0]
    taps = short_filter.shape[0]
    seqs, shards = sizes
    assert genomes == 1 and med_filter.shape == (PART, half // 16) and taps <= EDGE and ROWS < rows <= 2 * ROWS
    query, key, value, stream = (a.reshape(count, width) for a in (query, key, value, stream))

    sds = jax.ShapeDtypeStruct
    vmem = pl.BlockSpec(memory_space=pltpu.VMEM)
    hbm = pl.BlockSpec(memory_space=pl.ANY)
    dma = pltpu.SemaphoreType.DMA
    query_grad, key_grad, value_grad, a_sum = pl.pallas_call(
        functools.partial(block_kernel, sizes),
        in_specs=[hbm] * 4 + [vmem] * 3 + [hbm, vmem],
        out_specs=[hbm] * 3 + [vmem],
        out_shape=[sds((count, width), bf16)] * 3 + [sds((8, own), f32)],
        scratch_shapes=[
            pltpu.VMEM((count, width), bf16), pltpu.VMEM((count, width), bf16), pltpu.VMEM((count, width), bf16),
            pltpu.VMEM((count, width), bf16), pltpu.VMEM((own, half), bf16), pltpu.VMEM((3, count, width), bf16),
            pltpu.VMEM((3, RIM, width), bf16), pltpu.VMEM((3, RIM, width), bf16),
            pltpu.VMEM((2, 3, count + 2 * RIM, LANES), f32),
            pltpu.VMEM((2, rows, half), bf16), pltpu.VMEM((2, rows, half), bf16),
            pltpu.VMEM((PART, half), bf16), pltpu.VMEM((PART, half), bf16),
            pltpu.VMEM((far, half), bf16), pltpu.VMEM((far, half), bf16),
            pltpu.VMEM((2, rows, half), f32), pltpu.VMEM((2, rows, half), f32),
            pltpu.VMEM((2 * tiles, rows, LANES), f32),
            pltpu.VMEM((2, half // PART, 8 * ROWS, 2 * PART), bf16),
            pltpu.VMEM((2, count + far, LANES), bf16),
            pltpu.VMEM((2 * tiles, count, LANES), bf16),
            pltpu.VMEM((count, PART), f32), pltpu.VMEM((count, 16), f32),
            pltpu.VMEM((far, 16), f32), pltpu.VMEM((far, 16), f32),
            pltpu.VMEM((8, half), f32), pltpu.VMEM((shards, 8, own), f32), pltpu.VMEM((8, half), f32),
            pltpu.VMEM((2, 48, half), bf16), pltpu.VMEM((2, 32, half), bf16), pltpu.VMEM((2, count + far, 48), bf16),
            pltpu.VMEM((PART, LANES), f32),
            pltpu.VMEM((2, 1, rows, LANES), f32), pltpu.VMEM((2, 3, rows, LANES), f32),
            pltpu.VMEM((8, half), f32), pltpu.VMEM((shards, 8, own), f32), pltpu.VMEM((seqs, 8, own), f32),
            pltpu.VMEM((8, own), f32),
            dma((5,)), dma((3, 2 * tiles)), dma((2, 3)), dma((2, 3)), dma((2, tiles)), dma((2, tiles)), dma((2, tiles)), dma((2, tiles)),
            dma((2,)), dma((2,)), dma((shards,)), dma((shards,)), dma((shards,)), dma((shards,)),
            dma((seqs,)), dma((seqs,)),
        ],
        compiler_params=pltpu.CompilerParams(collective_id=0, has_side_effects=True, vmem_limit_bytes=VMEM_LIMIT),
        cost_estimate=pl.CostEstimate(flops=1024 * count * width * 8, bytes_accessed=20 * count * width, transcendentals=0),
        name="hyena_block",
    )(query, key, value, stream, targets, short_filter.transpose(1, 0, 2), med_filter, out_weight, head)

    steps = own // 128
    piece = pl.BlockSpec((count, width // steps), lambda i: (0, i))
    query_grad, key_grad, value_grad, out_grad = pl.pallas_call(
        finish_kernel,
        grid=(steps,),
        in_specs=[pl.BlockSpec((8, 128), lambda i: (0, i)), pl.BlockSpec((NUC, half), lambda i: (0, 0))] + [piece] * 3,
        out_specs=[piece] * 3 + [pl.BlockSpec((128, half), lambda i: (i, 0))],
        out_shape=[sds((count, width), bf16)] * 3 + [sds((own, half), f32)],
        scratch_shapes=[pltpu.VMEM((8, half), f32)],
        compiler_params=pltpu.CompilerParams(vmem_limit_bytes=VMEM_LIMIT // 2),
        name="finish",
    )(a_sum, head, query_grad, key_grad, value_grad)
    return (query_grad[None], key_grad[None], value_grad[None], out_grad)


def solution(mesh):
    rows = P("fsdp", "seq", None)
    return jax.shard_map(
        functools.partial(per_device, (mesh.shape["seq"], mesh.shape["fsdp"])),
        mesh=mesh,
        in_specs=(rows, rows, rows, rows, P("fsdp", "seq"), P(), P(), P("fsdp", None), P()),
        out_specs=(rows, rows, rows, P("fsdp", None)),
        check_vma=False,
    )
```

```python
import functools

import jax
import jax.numpy as jnp
from jax import lax
from jax.experimental import pallas as pl
from jax.experimental.pallas import tpu as pltpu
from jax.sharding import PartitionSpec as P

loss_scale = 64.0
LANES = 256
PART = 128
EDGE = 8
RIM = 16
ROWS = 96
NUC = 4
MESH = pl.DeviceIdType.MESH
VMEM_LIMIT = 58 * 1024 * 1024
f32, bf16 = jnp.float32, jnp.bfloat16


def split_bf16(x):
    high = x.astype(bf16)
    low = (x - high.astype(f32)).astype(bf16)
    return high, low


def mm(a, b, ca=1, cb=0):
    return lax.dot_general(a, b, (((ca,), (cb,)), ((), ())), preferred_element_type=f32)


def short_conv(taps, ref, at, size, later):
    first, step = (at, 1) if later else (at - EDGE, -1)
    near = far = None
    for j in range(4):
        moved = ref[first + step * j : first + step * j + size + EDGE, :]
        term = taps[j] * (moved[:size] if later else moved[EDGE:])
        near = term if near is None else near + term
        if j + 4 < len(taps):
            term = taps[j + 4] * moved
            far = term if far is None else far + term
    return near + far[4 : 4 + size]


def placed(size, reverse, source):
    r = lax.broadcasted_iota(jnp.int32, (size, 16), 0)
    c = lax.broadcasted_iota(jnp.int32, (size, 16), 1)
    v = r % 16
    row = (3 - v if reverse else v) + source(r // 16)
    return jnp.where((v < 4) & (c == row), 1.0, 0.0).astype(bf16)


def block_kernel(
    sizes, q_hbm, k_hbm, v_hbm, stream_hbm, target_ref, taps_ref, med_ref, w_hbm, head_ref,
    qo_ref, ko_ref, vo_ref, a_ref,
    q_ref, k_ref, v_ref, stream_ref, w_ref, done,
    rim_low, rim_high, raw, gate, prod, prod_low, prod_high, gate_low, gate_high, feat_k, feat_v, mix, toep,
    x, gated_s, logits, lg, lg_low, lg_high, head8, m_all, m_full, m_cat, n_cat, coef, grads, pg, feat, a_own, a_in,
    b_in, b_own,
    in_sems, out_sems, rim_ss, rim_rs, prod_ss, prod_rs, gate_ss, gate_rs, lg_ss, lg_rs, m_ss, m_rs, a_ss, a_rs,
    b_ss, b_rs,
):
    seqs, shards = sizes
    s, f = lax.axis_index("seq"), lax.axis_index("fsdp")
    count, width = q_ref.shape
    half = width // 2
    tiles = half // LANES
    rows = gate.shape[1]
    far = gate_low.shape[0]
    taps_n = taps_ref.shape[1]
    own = w_ref.shape[0]
    has_left, has_right = s > 0, s < seqs - 1
    loads = [
        pltpu.make_async_copy(src, dst, in_sems.at[i])
        for i, (src, dst) in enumerate(
            ((w_hbm, w_ref), (q_hbm, q_ref), (k_hbm, k_ref), (v_hbm, v_ref), (stream_hbm, stream_ref)))
    ]
    for load in loads:
        load.start()
    left, right = (s - 1, f), (s + 1, f)

    def seq_peer(d):
        return lax.rem(s + d, seqs)

    def shard_peer(d):
        return lax.rem(f + d, shards)

    barrier = pltpu.get_barrier_semaphore()
    for d in range(1, seqs):
        pl.semaphore_signal(barrier, inc=1, device_id=(seq_peer(d), f), device_id_type=MESH)
    for d in range(1, shards):
        pl.semaphore_signal(barrier, inc=1, device_id=(s, shard_peer(d)), device_id_type=MESH)
    pl.semaphore_wait(barrier, seqs + shards - 2)

    def send(src, dst, ss, rs, to):
        return pltpu.make_async_remote_copy(src_ref=src, dst_ref=dst, send_sem=ss, recv_sem=rs, device_id=to,
                                            device_id_type=MESH)

    def cols(t):
        return pl.ds(pl.multiple_of(t * LANES, LANES), LANES)

    def rim_copy(side, m):
        ref = (q_hbm, k_hbm, v_hbm)[m]
        if side == 0:
            return send(ref.at[count - RIM :], rim_low.at[m], rim_ss.at[side, m], rim_rs.at[side, m], right)
        return send(ref.at[:RIM], rim_high.at[m], rim_ss.at[side, m], rim_rs.at[side, m], left)

    def prod_copy(side, t):
        if side == 0:
            return send(prod.at[0, count - PART : count, cols(t)], prod_low.at[:, cols(t)], prod_ss.at[side, t],
                        prod_rs.at[side, t], right)
        return send(prod.at[1, rows - count : rows - count + PART, cols(t)], prod_high.at[:, cols(t)],
                    prod_ss.at[side, t], prod_rs.at[side, t], left)

    def gate_copy(side, t):
        if side == 0:
            return send(gate.at[1, rows - far :, cols(t)], gate_low.at[:, cols(t)], gate_ss.at[side, t],
                        gate_rs.at[side, t], right)
        return send(gate.at[0, :far, cols(t)], gate_high.at[:, cols(t)], gate_ss.at[side, t], gate_rs.at[side, t], left)

    def lg_copy(side):
        if side == 0:
            return send(lg.at[count - far :], lg_low, lg_ss.at[side], lg_rs.at[side], right)
        return send(lg.at[:far], lg_high, lg_ss.at[side], lg_rs.at[side], left)

    sends = (has_right, has_left)
    gets = (has_left, has_right)

    def start(side, copy):
        pl.when(sends[side])(lambda: copy.start())

    def sent(side, copy):
        pl.when(sends[side])(lambda: copy.wait_send())

    def arrived(side, copy):
        pl.when(gets[side])(lambda: copy.wait_recv())

    def clear(refs, absent):
        @pl.when(absent)
        def _():
            for ref in refs:
                ref[...] = jnp.zeros_like(ref)

    for side in (0, 1):
        for m in range(3):
            start(side, rim_copy(side, m))
    clear((rim_low, prod_low, gate_low, lg_low), s == 0)
    clear((rim_high, prod_high, gate_high, lg_high), s == seqs - 1)

    head8[...] = jnp.zeros_like(head8)
    head8[: head_ref.shape[0]] = head_ref[...]

    def stacked(value):
        high, low = split_bf16(value)
        return jnp.concatenate([high.astype(f32), low.astype(f32)], axis=0).astype(bf16)

    h_cat = stacked(head8[...])
    loads[0].wait()
    both = mm(h_cat, w_ref[...], 1, 1)
    m_all[f] = both[:8] + both[8:]

    def m_copy(d, slot):
        return send(m_all.at[f], m_all.at[slot], m_ss.at[d - 1], m_rs.at[slot], (s, shard_peer(d)))

    for d in range(1, shards):
        m_copy(d, f).start()

    med = med_ref[...]
    tap = lax.broadcasted_iota(jnp.int32, (PART, 2 * PART), 0)
    place = lax.broadcasted_iota(jnp.int32, (PART, 2 * PART), 1)
    for o, here in enumerate((place == PART - tap, place == tap)):
        grads[:PART, :] = mm(med, jnp.where(here, 1.0, 0.0).astype(bf16), 0, 0)

        @pl.loop(0, toep.shape[1])
        def _(i):
            base = grads[pl.ds(pl.multiple_of(i * 8, 8), 8), :]
            for g in range(8):
                row = jnp.broadcast_to(base[g : g + 1, :], (RIM, 2 * PART))
                strip = pltpu.roll(row, 0, 1, stride=1, stride_axis=0).astype(bf16)
                for k in range(0, ROWS, RIM):
                    toep[o, i, g * ROWS + k : g * ROWS + k + RIM, :] = pltpu.roll(strip, k, 1) if k else strip

    def banded(o, t, x, out_ref, slot):
        span = ROWS + PART
        late = rows - ROWS
        lane = lax.rem(lax.broadcasted_iota(jnp.int32, (1, 2 * PART), 1), PART) // (PART // 8)
        for part in range(LANES // PART):
            here = slice(part * PART, (part + 1) * PART)
            two = jnp.concatenate([x[:span, here], x[late : late + span, here]], axis=1)
            every = mm(toep[o, t * (LANES // PART) + part, :, :span], two)
            got = every[:ROWS]
            for g in range(1, 8):
                got = jnp.where(lane == g, every[g * ROWS : (g + 1) * ROWS], got)
            out_ref[slot, :ROWS, here] = got[:, :PART]
            out_ref[slot, late:, here] = got[:, PART:]

    def low_half(i):
        return jnp.where(i == 1, 8, 0)

    for h in (0, 1):
        n_cat[h] = mm(placed(32, h == 1, low_half), h_cat).astype(bf16)

    for load in loads[1:]:
        load.wait()
    for side in (0, 1):
        for m in range(3):
            arrived(side, rim_copy(side, m))

    for h in (0, 1):
        def featured(t, raw):
            for part in range(LANES // PART):
                there = pl.ds(pl.multiple_of(h * half + t * LANES + part * PART, PART), PART)
                here = pl.ds(pl.multiple_of(t * LANES + part * PART, PART), PART)
                for m, ref in enumerate((q_ref, k_ref, v_ref)):
                    raw[m, part, :RIM] = rim_low[m, :, there].astype(f32)
                    raw[m, part, RIM : RIM + count] = ref[:, there].astype(f32)
                    raw[m, part, RIM + count :] = rim_high[m, :, there].astype(f32)
                taps = [[taps_ref[m, j : j + 1, here] for j in range(taps_n)] for m in range(3)]
                for at, size in ((0, ROWS), (ROWS, rows - ROWS)):
                    feats = [short_conv(taps[m], raw.at[m, part], at + (0 if h else RIM), size, h == 1) for m in range(3)]
                    gate[h, at : at + size, here] = feats[0].astype(bf16)
                    feat_k[h, at : at + size, here] = feats[1]
                    feat_v[h, at : at + size, here] = feats[2]
                    prod[h, at : at + size, here] = (feats[1] * feats[2]).astype(bf16)

        @pl.loop(0, tiles // 2)
        def _(i):
            for u in (0, 1):
                featured(2 * i + u, raw.at[u])
            for u in (0, 1):
                start(h, prod_copy(h, 2 * i + u))
                start(1 - h, gate_copy(1 - h, 2 * i + u))

    for d in range(1, shards):
        m_copy(d, shard_peer(d)).wait_recv()
    for p in range(shards):
        m_full[:, p * own : (p + 1) * own] = m_all[p]
    both_m = stacked(m_full[...])
    for h in (0, 1):
        m_cat[h] = mm(placed(48, h == 1, low_half), both_m).astype(bf16)

    logits[...] = jnp.zeros_like(logits)
    for h in (0, 1):

        def mixed(t, x):
            if h:
                x[:rows] = prod[1, :, cols(t)]
                x[rows:] = prod_high[:, cols(t)]
            else:
                x[:PART] = prod_low[:, cols(t)]
                x[PART:] = prod[0, :, cols(t)]
            banded(h, t, x, mix, h * tiles + t)
            first = rows - count if h else 0
            gated = (gate[h, first : first + count, cols(t)].astype(f32)
                     * mix[h * tiles + t, first : first + count, :]).astype(bf16)
            gated_s[h * tiles + t] = gated
            stream = stream_ref[:, pl.ds(pl.multiple_of(h * half + t * LANES, LANES), LANES)]
            return mm(gated, m_cat[h, :32, cols(t)], 1, 1) + mm(stream, n_cat[h, :, cols(t)], 1, 1)

        @pl.loop(0, tiles // 2)
        def _(i):
            for u in (0, 1):
                arrived(h, prod_copy(h, 2 * i + u))
            one, two = (mixed(2 * i + u, x.at[u]) for u in (0, 1))
            logits[:, :32] += one + two

    sums = logits[...]
    sums = (sums + pltpu.roll(sums, PART - 16, 1))[:, :16]
    lane = lax.broadcasted_iota(jnp.int32, sums.shape, 1)
    hot = lax.broadcasted_iota(jnp.int32, (16, count), 0) == target_ref[...]
    hot = jnp.where(hot, 1.0, 0.0).astype(bf16)
    eye = lax.broadcasted_iota(jnp.int32, (16, 16), 0) == lax.broadcasted_iota(jnp.int32, (16, 16), 1)
    one_hot = mm(hot, jnp.where(eye, 1.0, 0.0).astype(bf16), 0, 0)
    exponent = jnp.where(lane < 4, jnp.exp(sums), 0.0)
    softmax_out = exponent / jnp.sum(exponent, axis=1, keepdims=True)
    grad = loss_scale * (softmax_out - one_hot)
    lg[...] = grad
    for side in (0, 1):
        start(side, lg_copy(side))

    g_high, g_low = split_bf16(grad)
    swap = (lax.broadcasted_iota(jnp.int32, (16, 16), 0) + lax.broadcasted_iota(jnp.int32, (16, 16), 1)) == 3
    swap = jnp.where(swap, 1.0, 0.0).astype(bf16)
    r_high, r_low = mm(g_high, swap).astype(bf16), mm(g_low, swap).astype(bf16)

    @pl.loop(0, tiles)
    def _(t):
        one, two = gated_s[t], gated_s[tiles + t]
        total = (mm(g_high, one, 0, 0) + mm(g_low, one, 0, 0)) + (mm(r_high, two, 0, 0) + mm(r_low, two, 0, 0))
        a_own[:, cols(t)] = total[:8]

    def a_copy(d, slot):
        p = shard_peer(d)
        return send(a_own.at[:, pl.ds(pl.multiple_of(p * own, 128), own)], a_in.at[slot], a_ss.at[d - 1],
                    a_rs.at[slot], (s, p))

    def b_copy(d, slot):
        return send(b_own, b_in.at[slot], b_ss.at[d - 1], b_rs.at[slot], (seq_peer(d), f))

    for d in range(1, shards):
        a_copy(d, f).start()

    spot = lax.broadcasted_iota(jnp.int32, (16, 48), 1)
    lane48 = lax.broadcasted_iota(jnp.int32, (16, 48), 0)
    to_high = jnp.where((spot == lane48) | (spot == lane48 + 16), 1.0, 0.0).astype(bf16)
    to_low = jnp.where(spot == lane48 + 32, 1.0, 0.0).astype(bf16)

    def spread(value):
        high, low = split_bf16(value)
        return (mm(high, to_high) + mm(low, to_low)).astype(bf16)

    local = spread(lg[...])
    coef[0, :count] = local
    coef[1, far:] = local
    for side in (0, 1):
        arrived(side, lg_copy(side))
    coef[0, count:] = spread(lg_high[...])
    coef[1, :far] = spread(lg_low[...])

    def out_copy(m, h, t):
        there = pl.ds(pl.multiple_of(h * half + t * LANES, LANES), LANES)
        return pltpu.make_async_copy(done.at[m, :, there], (qo_ref, ko_ref, vo_ref)[m].at[:, there],
                                     out_sems.at[m, h * tiles + t])

    for h in (0, 1):

        def backward(t, x, grads, pg, feat):
            part = mm(coef[h], m_cat[h, :, cols(t)])
            if h:
                factors = ((0, far, gate_low[:, cols(t)]), (far, count, gate[1, rows - count :, cols(t)]))
            else:
                factors = ((0, count, gate[0, :count, cols(t)]), (count, far, gate_high[:, cols(t)]))
            for at, size, factor in factors:
                x[at : at + size] = (part[at : at + size] * factor.astype(f32)).astype(bf16)
            mine = count + far - rows if h else 0
            for c in range(LANES // PART):
                lanes = slice(c * PART, (c + 1) * PART)
                feat[0, c] = part[mine : mine + rows, lanes] * mix[h * tiles + t, :, lanes]
            banded(1 - h, t, x, pg, 0)
            for c in range(LANES // PART):
                lanes = slice(c * PART, (c + 1) * PART)
                here = pl.ds(pl.multiple_of(t * LANES + c * PART, PART), PART)
                there = pl.ds(pl.multiple_of(h * half + t * LANES + c * PART, PART), PART)
                feat[1, c] = pg[0, :, lanes] * feat_v[h, :, here]
                feat[2, c] = pg[0, :, lanes] * feat_k[h, :, here]
                size = count // 2
                for m in range(3):
                    taps = [taps_ref[m, j : j + 1, here] for j in range(taps_n)]
                    for at in (0, size):
                        got = short_conv(taps, feat.at[m, c], at + (RIM if h else 0), size, h == 0)
                        done[m, at : at + size, there] = got.astype(bf16)

        @pl.loop(0, tiles // 2)
        def _(i):
            for u in (0, 1):
                arrived(1 - h, gate_copy(1 - h, 2 * i + u))
            for u in (0, 1):
                backward(2 * i + u, x.at[u], grads, pg.at[u], feat.at[u])
            for u in (0, 1):
                for m in range(3):
                    out_copy(m, h, 2 * i + u).start()

        if h == 0:
            total = a_own[:, pl.ds(pl.multiple_of(f * own, 128), own)]
            for d in range(1, shards):
                a_copy(d, shard_peer(d)).wait_recv()
                total = total + a_in[shard_peer(d)]
            b_own[...] = total
            for d in range(1, seqs):
                b_copy(d, s).start()

    total = b_own[...]
    for d in range(1, seqs):
        b_copy(d, seq_peer(d)).wait_recv()
        total = total + b_in[seq_peer(d)]
    a_ref[...] = total * (1.0 / loss_scale)

    @pl.loop(0, tiles)
    def _(t):
        for h in (0, 1):
            for m in range(3):
                out_copy(m, h, t).wait()

    for side in (0, 1):
        for m in range(3):
            sent(side, rim_copy(side, m))
        sent(side, lg_copy(side))

        @pl.loop(0, tiles)
        def _(t):
            sent(side, prod_copy(side, t))
            sent(side, gate_copy(side, t))

    for d in range(1, shards):
        m_copy(d, f).wait_send()
        a_copy(d, f).wait_send()
    for d in range(1, seqs):
        b_copy(d, s).wait_send()


def finish_kernel(a_ref, head_ref, q_ref, k_ref, v_ref, qo_ref, ko_ref, vo_ref, out_ref, head8):
    @pl.when(pl.program_id(0) == 0)
    def _():
        head8[...] = jnp.zeros_like(head8)
        head8[: head_ref.shape[0]] = head_ref[...]

    for src, dst in ((q_ref, qo_ref), (k_ref, ko_ref), (v_ref, vo_ref)):
        dst[...] = src[...]
    a_high, a_low = split_bf16(a_ref[...])
    h_high, h_low = split_bf16(head8[...])
    out_ref[...] = mm(a_high, h_high, 0, 0) + (mm(a_high, h_low, 0, 0) + mm(a_low, h_high, 0, 0))


def per_device(sizes, query, key, value, stream, targets, short_filter, med_filter, out_weight, head):
    genomes, count, width = query.shape
    half = width // 2
    tiles = half // LANES
    rows = count + 2 * EDGE
    far = count - RIM
    own = out_weight.shape[0]
    taps = short_filter.shape[0]
    seqs, shards = sizes
    assert genomes == 1 and med_filter.shape == (PART, half // 16) and 4 < taps <= EDGE and count % 32 == 0 and ROWS < rows <= 2 * ROWS
    query, key, value, stream = (a.reshape(count, width) for a in (query, key, value, stream))

    sds = jax.ShapeDtypeStruct
    vmem = pl.BlockSpec(memory_space=pltpu.VMEM)
    hbm = pl.BlockSpec(memory_space=pl.ANY)
    dma = pltpu.SemaphoreType.DMA
    query_grad, key_grad, value_grad, a_sum = pl.pallas_call(
        functools.partial(block_kernel, sizes),
        in_specs=[hbm] * 4 + [vmem] * 3 + [hbm, vmem],
        out_specs=[hbm] * 3 + [vmem],
        out_shape=[sds((count, width), bf16)] * 3 + [sds((8, own), f32)],
        scratch_shapes=[
            pltpu.VMEM((count, width), bf16), pltpu.VMEM((count, width), bf16), pltpu.VMEM((count, width), bf16),
            pltpu.VMEM((count, width), bf16), pltpu.VMEM((own, half), bf16), pltpu.VMEM((3, count, width), bf16),
            pltpu.VMEM((3, RIM, width), bf16), pltpu.VMEM((3, RIM, width), bf16),
            pltpu.VMEM((2, 3, LANES // PART, count + 2 * RIM, PART), f32),
            pltpu.VMEM((2, rows, half), bf16), pltpu.VMEM((2, rows, half), bf16),
            pltpu.VMEM((PART, half), bf16), pltpu.VMEM((PART, half), bf16),
            pltpu.VMEM((far, half), bf16), pltpu.VMEM((far, half), bf16),
            pltpu.VMEM((2, rows, half), f32), pltpu.VMEM((2, rows, half), f32),
            pltpu.VMEM((2 * tiles, rows, LANES), f32),
            pltpu.VMEM((2, half // PART, 8 * ROWS, 2 * PART), bf16),
            pltpu.VMEM((2, count + far, LANES), bf16),
            pltpu.VMEM((2 * tiles, count, LANES), bf16),
            pltpu.VMEM((count, PART), f32), pltpu.VMEM((count, 16), f32),
            pltpu.VMEM((far, 16), f32), pltpu.VMEM((far, 16), f32),
            pltpu.VMEM((8, half), f32), pltpu.VMEM((shards, 8, own), f32), pltpu.VMEM((8, half), f32),
            pltpu.VMEM((2, 48, half), bf16), pltpu.VMEM((2, 32, half), bf16), pltpu.VMEM((2, count + far, 48), bf16),
            pltpu.VMEM((PART, LANES), f32),
            pltpu.VMEM((2, 1, rows, LANES), f32), pltpu.VMEM((2, 3, LANES // PART, rows, PART), f32),
            pltpu.VMEM((8, half), f32), pltpu.VMEM((shards, 8, own), f32), pltpu.VMEM((seqs, 8, own), f32),
            pltpu.VMEM((8, own), f32),
            dma((5,)), dma((3, 2 * tiles)), dma((2, 3)), dma((2, 3)), dma((2, tiles)), dma((2, tiles)), dma((2, tiles)), dma((2, tiles)),
            dma((2,)), dma((2,)), dma((shards,)), dma((shards,)), dma((shards,)), dma((shards,)),
            dma((seqs,)), dma((seqs,)),
        ],
        compiler_params=pltpu.CompilerParams(collective_id=0, has_side_effects=True, vmem_limit_bytes=VMEM_LIMIT),
        cost_estimate=pl.CostEstimate(flops=1024 * count * width * 8, bytes_accessed=20 * count * width, transcendentals=0),
        name="hyena_block",
    )(query, key, value, stream, targets, short_filter.transpose(1, 0, 2), med_filter, out_weight, head)

    steps = own // 128
    piece = pl.BlockSpec((count, width // steps), lambda i: (0, i))
    query_grad, key_grad, value_grad, out_grad = pl.pallas_call(
        finish_kernel,
        grid=(steps,),
        in_specs=[pl.BlockSpec((8, 128), lambda i: (0, i)), pl.BlockSpec((NUC, half), lambda i: (0, 0))] + [piece] * 3,
        out_specs=[piece] * 3 + [pl.BlockSpec((128, half), lambda i: (i, 0))],
        out_shape=[sds((count, width), bf16)] * 3 + [sds((own, half), f32)],
        scratch_shapes=[pltpu.VMEM((8, half), f32)],
        compiler_params=pltpu.CompilerParams(vmem_limit_bytes=VMEM_LIMIT),
        name="finish",
    )(a_sum, head, query_grad, key_grad, value_grad)
    return (query_grad[None], key_grad[None], value_grad[None], out_grad)


def solution(mesh):
    rows = P("fsdp", "seq", None)
    return jax.shard_map(
        functools.partial(per_device, (mesh.shape["seq"], mesh.shape["fsdp"])),
        mesh=mesh,
        in_specs=(rows, rows, rows, rows, P("fsdp", "seq"), P(), P(), P("fsdp", None), P()),
        out_specs=(rows, rows, rows, P("fsdp", None)),
        check_vma=False,
    )
```

```python
import functools

import jax
import jax.numpy as jnp
from jax import lax
from jax.experimental import pallas as pl
from jax.experimental.pallas import tpu as pltpu
from jax.sharding import PartitionSpec as P

loss_scale = 64.0
LANES = 256
PART = 128
EDGE = 8
RIM = 16
ROWS = 96
NUC = 4
MESH = pl.DeviceIdType.MESH
VMEM_LIMIT = 58 * 1024 * 1024
f32, bf16 = jnp.float32, jnp.bfloat16


def split_bf16(x):
    high = x.astype(bf16)
    low = (x - high.astype(f32)).astype(bf16)
    return high, low


def mm(a, b, ca=1, cb=0):
    return lax.dot_general(a, b, (((ca,), (cb,)), ((), ())), preferred_element_type=f32)


def short_conv(taps, ref, at, size, later):
    first, step = (at, 1) if later else (at - EDGE, -1)
    near = far = None
    for j in range(4):
        moved = ref[first + step * j : first + step * j + size + EDGE, :]
        term = taps[j] * (moved[:size] if later else moved[EDGE:])
        near = term if near is None else near + term
        if j + 4 < len(taps):
            term = taps[j + 4] * moved
            far = term if far is None else far + term
    return near + far[4 : 4 + size]


def placed(size, reverse, source):
    r = lax.broadcasted_iota(jnp.int32, (size, 16), 0)
    c = lax.broadcasted_iota(jnp.int32, (size, 16), 1)
    v = r % 16
    row = (3 - v if reverse else v) + source(r // 16)
    return jnp.where((v < 4) & (c == row), 1.0, 0.0).astype(bf16)


def block_kernel(
    sizes, q_hbm, k_hbm, v_hbm, stream_hbm, target_ref, taps_ref, med_ref, w_hbm, head_ref,
    qo_ref, ko_ref, vo_ref, a_ref,
    q_ref, k_ref, v_ref, stream_ref, w_ref, done,
    edges, kv_out, q_low, q_high, kv_low, kv_high, raw, gate, prod, prod_low, prod_high, gate_low, gate_high, feat_k, feat_v, mix, toep,
    x, gated_s, logits, lg, lg_low, lg_high, head8, m_all, m_full, m_cat, n_cat, coef, grads, pg, feat, a_own, a_in,
    b_in, b_own,
    edge_sems, in_sems, out_sems, rim_ss, rim_rs, prod_ss, prod_rs, gate_ss, gate_rs, lg_ss, lg_rs, m_ss, m_rs, a_ss, a_rs,
    b_ss, b_rs,
):
    seqs, shards = sizes
    s, f = lax.axis_index("seq"), lax.axis_index("fsdp")
    count, width = q_ref.shape
    half = width // 2
    tiles = half // LANES
    rows = gate.shape[1]
    far = gate_low.shape[0]
    taps_n = taps_ref.shape[1]
    own = w_ref.shape[0]
    has_left, has_right = s > 0, s < seqs - 1
    ends = [
        pltpu.make_async_copy(src, edges.at[i], edge_sems.at[i])
        for i, src in enumerate((k_hbm.at[count - RIM :], v_hbm.at[count - RIM :], k_hbm.at[:RIM], v_hbm.at[:RIM]))
    ]
    for end in ends:
        end.start()
    loads = [
        pltpu.make_async_copy(src, dst, in_sems.at[i])
        for i, (src, dst) in enumerate(
            ((w_hbm, w_ref), (q_hbm, q_ref), (k_hbm, k_ref), (v_hbm, v_ref), (stream_hbm, stream_ref)))
    ]
    for load in loads:
        load.start()
    left, right = (s - 1, f), (s + 1, f)

    def seq_peer(d):
        return lax.rem(s + d, seqs)

    def shard_peer(d):
        return lax.rem(f + d, shards)

    barrier = pltpu.get_barrier_semaphore()
    for d in range(1, seqs):
        pl.semaphore_signal(barrier, inc=1, device_id=(seq_peer(d), f), device_id_type=MESH)
    for d in range(1, shards):
        pl.semaphore_signal(barrier, inc=1, device_id=(s, shard_peer(d)), device_id_type=MESH)
    pl.semaphore_wait(barrier, seqs + shards - 2)

    def send(src, dst, ss, rs, to):
        return pltpu.make_async_remote_copy(src_ref=src, dst_ref=dst, send_sem=ss, recv_sem=rs, device_id=to,
                                            device_id_type=MESH)

    def cols(t):
        return pl.ds(pl.multiple_of(t * LANES, LANES), LANES)

    def rim_copy(side, m):
        ss, rs, to = rim_ss.at[side, m], rim_rs.at[side, m], (right, left)[side]
        if m:
            return send(kv_out.at[side], (kv_low, kv_high)[side], ss, rs, to)
        if side == 0:
            return send(q_hbm.at[count - RIM :, :half], q_low, ss, rs, to)
        return send(q_hbm.at[:RIM, half:], q_high, ss, rs, to)

    def prod_copy(side, t):
        if side == 0:
            return send(prod.at[0, count - PART : count, cols(t)], prod_low.at[:, cols(t)], prod_ss.at[side, t],
                        prod_rs.at[side, t], right)
        return send(prod.at[1, rows - count : rows - count + PART, cols(t)], prod_high.at[:, cols(t)],
                    prod_ss.at[side, t], prod_rs.at[side, t], left)

    def gate_copy(side, t):
        if side == 0:
            return send(gate.at[1, rows - far :, cols(t)], gate_low.at[:, cols(t)], gate_ss.at[side, t],
                        gate_rs.at[side, t], right)
        return send(gate.at[0, :far, cols(t)], gate_high.at[:, cols(t)], gate_ss.at[side, t], gate_rs.at[side, t], left)

    def lg_copy(side):
        if side == 0:
            return send(lg.at[count - far :], lg_low, lg_ss.at[side], lg_rs.at[side], right)
        return send(lg.at[:far], lg_high, lg_ss.at[side], lg_rs.at[side], left)

    sends = (has_right, has_left)
    gets = (has_left, has_right)

    def start(side, copy):
        pl.when(sends[side])(lambda: copy.start())

    def sent(side, copy):
        pl.when(sends[side])(lambda: copy.wait_send())

    def arrived(side, copy):
        pl.when(gets[side])(lambda: copy.wait_recv())

    def clear(refs, absent):
        @pl.when(absent)
        def _():
            for ref in refs:
                ref[...] = jnp.zeros_like(ref)

    for end in ends:
        end.wait()
    for side, rows_of in ((0, slice(RIM - EDGE, RIM)), (1, slice(0, EDGE))):
        pair = [edges[2 * side + i].astype(f32)[rows_of] for i in (0, 1)]
        kv_out[side] = jnp.concatenate(pair, axis=0).astype(bf16)
    for m in (1, 0):
        for side in (0, 1):
            start(side, rim_copy(side, m))
    clear((q_low, kv_low, prod_low, gate_low, lg_low), s == 0)
    clear((q_high, kv_high, prod_high, gate_high, lg_high), s == seqs - 1)
    raw[...] = jnp.zeros_like(raw)

    head8[...] = jnp.zeros_like(head8)
    head8[: head_ref.shape[0]] = head_ref[...]

    def stacked(value):
        high, low = split_bf16(value)
        return jnp.concatenate([high.astype(f32), low.astype(f32)], axis=0).astype(bf16)

    h_cat = stacked(head8[...])
    loads[0].wait()
    both = mm(h_cat, w_ref[...], 1, 1)
    m_all[f] = both[:8] + both[8:]

    def m_copy(d, slot):
        return send(m_all.at[f], m_all.at[slot], m_ss.at[d - 1], m_rs.at[slot], (s, shard_peer(d)))

    for d in range(1, shards):
        m_copy(d, f).start()

    med = med_ref[...]
    tap = lax.broadcasted_iota(jnp.int32, (PART, 2 * PART), 0)
    place = lax.broadcasted_iota(jnp.int32, (PART, 2 * PART), 1)
    for o, here in enumerate((place == PART - tap, place == tap)):
        grads[:PART, :] = mm(med, jnp.where(here, 1.0, 0.0).astype(bf16), 0, 0)

        @pl.loop(0, toep.shape[1])
        def _(i):
            base = grads[pl.ds(pl.multiple_of(i * 8, 8), 8), :]
            for g in range(8):
                row = jnp.broadcast_to(base[g : g + 1, :], (RIM, 2 * PART))
                strip = pltpu.roll(row, 0, 1, stride=1, stride_axis=0).astype(bf16)
                for k in range(0, ROWS, RIM):
                    toep[o, i, g * ROWS + k : g * ROWS + k + RIM, :] = pltpu.roll(strip, k, 1) if k else strip

    def banded(o, t, x, out_ref, slot):
        span = ROWS + PART
        late = rows - ROWS
        lane = lax.rem(lax.broadcasted_iota(jnp.int32, (1, 2 * PART), 1), PART) // (PART // 8)
        for part in range(LANES // PART):
            here = slice(part * PART, (part + 1) * PART)
            two = jnp.concatenate([x[:span, here], x[late : late + span, here]], axis=1)
            every = mm(toep[o, t * (LANES // PART) + part, :, :span], two)
            got = every[:ROWS]
            for g in range(1, 8):
                got = jnp.where(lane == g, every[g * ROWS : (g + 1) * ROWS], got)
            out_ref[slot, :ROWS, here] = got[:, :PART]
            out_ref[slot, late:, here] = got[:, PART:]

    def low_half(i):
        return jnp.where(i == 1, 8, 0)

    for h in (0, 1):
        n_cat[h] = mm(placed(32, h == 1, low_half), h_cat).astype(bf16)

    for load in loads[1:]:
        load.wait()
    for side in (0, 1):
        for m in range(2):
            arrived(side, rim_copy(side, m))

    for h in (0, 1):
        def featured(t, raw):
            for part in range(LANES // PART):
                there = pl.ds(pl.multiple_of(h * half + t * LANES + part * PART, PART), PART)
                here = pl.ds(pl.multiple_of(t * LANES + part * PART, PART), PART)
                end = RIM + count
                if h:
                    raw[0, part, end:] = q_high[:, here].astype(f32)
                else:
                    raw[0, part, :RIM] = q_low[:, here].astype(f32)
                low, high = kv_low[:, there].astype(f32), kv_high[:, there].astype(f32)
                for m in (1, 2):
                    raw[m, part, RIM - EDGE : RIM] = low[(m - 1) * EDGE : m * EDGE]
                    raw[m, part, end : end + EDGE] = high[(m - 1) * EDGE : m * EDGE]
                for m, ref in enumerate((q_ref, k_ref, v_ref)):
                    raw[m, part, RIM:end] = ref[:, there].astype(f32)
                taps = [[taps_ref[m, j : j + 1, here] for j in range(taps_n)] for m in range(3)]
                for at, size in ((0, ROWS), (ROWS, rows - ROWS)):
                    feats = [short_conv(taps[m], raw.at[m, part], at + (0 if h else RIM), size, h == 1) for m in range(3)]
                    gate[h, at : at + size, here] = feats[0].astype(bf16)
                    feat_k[h, at : at + size, here] = feats[1]
                    feat_v[h, at : at + size, here] = feats[2]
                    prod[h, at : at + size, here] = (feats[1] * feats[2]).astype(bf16)

        @pl.loop(0, tiles // 2)
        def _(i):
            for u in (0, 1):
                featured(2 * i + u, raw.at[u])
            for u in (0, 1):
                start(h, prod_copy(h, 2 * i + u))

    for d in range(1, shards):
        m_copy(d, shard_peer(d)).wait_recv()
    for p in range(shards):
        m_full[:, p * own : (p + 1) * own] = m_all[p]
    both_m = stacked(m_full[...])
    for h in (0, 1):
        m_cat[h] = mm(placed(48, h == 1, low_half), both_m).astype(bf16)

    logits[...] = jnp.zeros_like(logits)
    for h in (0, 1):

        def mixed(t, x):
            if h:
                x[:rows] = prod[1, :, cols(t)]
                x[rows:] = prod_high[:, cols(t)]
            else:
                x[:PART] = prod_low[:, cols(t)]
                x[PART:] = prod[0, :, cols(t)]
            banded(h, t, x, mix, h * tiles + t)
            first = rows - count if h else 0
            gated = (gate[h, first : first + count, cols(t)].astype(f32)
                     * mix[h * tiles + t, first : first + count, :]).astype(bf16)
            gated_s[h * tiles + t] = gated
            stream = stream_ref[:, pl.ds(pl.multiple_of(h * half + t * LANES, LANES), LANES)]
            return mm(gated, m_cat[h, :32, cols(t)], 1, 1) + mm(stream, n_cat[h, :, cols(t)], 1, 1)

        @pl.loop(0, tiles // 2)
        def _(i):
            for u in (0, 1):
                arrived(h, prod_copy(h, 2 * i + u))
            for u in (0, 1):
                start(h, gate_copy(h, 2 * i + u))
            one, two = (mixed(2 * i + u, x.at[u]) for u in (0, 1))
            logits[:, :32] += one + two

    sums = logits[...]
    sums = (sums + pltpu.roll(sums, PART - 16, 1))[:, :16]
    lane = lax.broadcasted_iota(jnp.int32, sums.shape, 1)
    hot = lax.broadcasted_iota(jnp.int32, (16, count), 0) == target_ref[...]
    hot = jnp.where(hot, 1.0, 0.0).astype(bf16)
    eye = lax.broadcasted_iota(jnp.int32, (16, 16), 0) == lax.broadcasted_iota(jnp.int32, (16, 16), 1)
    one_hot = mm(hot, jnp.where(eye, 1.0, 0.0).astype(bf16), 0, 0)
    exponent = jnp.where(lane < 4, jnp.exp(sums), 0.0)
    softmax_out = exponent / jnp.sum(exponent, axis=1, keepdims=True)
    grad = loss_scale * (softmax_out - one_hot)
    lg[...] = grad
    for side in (0, 1):
        start(side, lg_copy(side))

    g_high, g_low = split_bf16(grad)
    swap = (lax.broadcasted_iota(jnp.int32, (16, 16), 0) + lax.broadcasted_iota(jnp.int32, (16, 16), 1)) == 3
    swap = jnp.where(swap, 1.0, 0.0).astype(bf16)
    r_high, r_low = mm(g_high, swap).astype(bf16), mm(g_low, swap).astype(bf16)

    @pl.loop(0, tiles)
    def _(t):
        one, two = gated_s[t], gated_s[tiles + t]
        total = (mm(g_high, one, 0, 0) + mm(g_low, one, 0, 0)) + (mm(r_high, two, 0, 0) + mm(r_low, two, 0, 0))
        a_own[:, cols(t)] = total[:8]

    def a_copy(d, slot):
        p = shard_peer(d)
        return send(a_own.at[:, pl.ds(pl.multiple_of(p * own, 128), own)], a_in.at[slot], a_ss.at[d - 1],
                    a_rs.at[slot], (s, p))

    def b_copy(d, slot):
        return send(b_own, b_in.at[slot], b_ss.at[d - 1], b_rs.at[slot], (seq_peer(d), f))

    for d in range(1, shards):
        a_copy(d, f).start()

    spot = lax.broadcasted_iota(jnp.int32, (16, 48), 1)
    lane48 = lax.broadcasted_iota(jnp.int32, (16, 48), 0)
    to_high = jnp.where((spot == lane48) | (spot == lane48 + 16), 1.0, 0.0).astype(bf16)
    to_low = jnp.where(spot == lane48 + 32, 1.0, 0.0).astype(bf16)

    def spread(value):
        high, low = split_bf16(value)
        return (mm(high, to_high) + mm(low, to_low)).astype(bf16)

    local = spread(lg[...])
    coef[0, :count] = local
    coef[1, far:] = local
    for side in (0, 1):
        arrived(side, lg_copy(side))
    coef[0, count:] = spread(lg_high[...])
    coef[1, :far] = spread(lg_low[...])

    def out_copy(m, h, t):
        there = pl.ds(pl.multiple_of(h * half + t * LANES, LANES), LANES)
        return pltpu.make_async_copy(done.at[m, :, there], (qo_ref, ko_ref, vo_ref)[m].at[:, there],
                                     out_sems.at[m, h * tiles + t])

    for h in (1, 0):

        def backward(t, x, grads, pg, feat):
            part = mm(coef[h], m_cat[h, :, cols(t)])
            if h:
                factors = ((0, far, gate_low[:, cols(t)]), (far, count, gate[1, rows - count :, cols(t)]))
            else:
                factors = ((0, count, gate[0, :count, cols(t)]), (count, far, gate_high[:, cols(t)]))
            for at, size, factor in factors:
                x[at : at + size] = (part[at : at + size] * factor.astype(f32)).astype(bf16)
            mine = count + far - rows if h else 0
            for c in range(LANES // PART):
                lanes = slice(c * PART, (c + 1) * PART)
                feat[0, c] = part[mine : mine + rows, lanes] * mix[h * tiles + t, :, lanes]
            banded(1 - h, t, x, pg, 0)
            for c in range(LANES // PART):
                lanes = slice(c * PART, (c + 1) * PART)
                here = pl.ds(pl.multiple_of(t * LANES + c * PART, PART), PART)
                there = pl.ds(pl.multiple_of(h * half + t * LANES + c * PART, PART), PART)
                feat[1, c] = pg[0, :, lanes] * feat_v[h, :, here]
                feat[2, c] = pg[0, :, lanes] * feat_k[h, :, here]
                size = count // 2
                for m in range(3):
                    taps = [taps_ref[m, j : j + 1, here] for j in range(taps_n)]
                    for at in (0, size):
                        got = short_conv(taps, feat.at[m, c], at + (RIM if h else 0), size, h == 0)
                        done[m, at : at + size, there] = got.astype(bf16)

        @pl.loop(0, tiles // 2)
        def _(i):
            for u in (0, 1):
                arrived(1 - h, gate_copy(1 - h, 2 * i + u))
            for u in (0, 1):
                backward(2 * i + u, x.at[u], grads, pg.at[u], feat.at[u])
            for u in (0, 1):
                for m in range(3):
                    out_copy(m, h, 2 * i + u).start()

        if h == 1:
            total = a_own[:, pl.ds(pl.multiple_of(f * own, 128), own)]
            for d in range(1, shards):
                a_copy(d, shard_peer(d)).wait_recv()
                total = total + a_in[shard_peer(d)]
            b_own[...] = total
            for d in range(1, seqs):
                b_copy(d, s).start()

    total = b_own[...]
    for d in range(1, seqs):
        b_copy(d, seq_peer(d)).wait_recv()
        total = total + b_in[seq_peer(d)]
    a_ref[...] = total * (1.0 / loss_scale)

    @pl.loop(0, tiles)
    def _(t):
        for h in (0, 1):
            for m in range(3):
                out_copy(m, h, t).wait()

    for side in (0, 1):
        for m in range(2):
            sent(side, rim_copy(side, m))
        sent(side, lg_copy(side))

        @pl.loop(0, tiles)
        def _(t):
            sent(side, prod_copy(side, t))
            sent(side, gate_copy(side, t))

    for d in range(1, shards):
        m_copy(d, f).wait_send()
        a_copy(d, f).wait_send()
    for d in range(1, seqs):
        b_copy(d, s).wait_send()


def finish_kernel(a_ref, head_ref, q_ref, k_ref, v_ref, qo_ref, ko_ref, vo_ref, out_ref, head8):
    @pl.when(pl.program_id(0) == 0)
    def _():
        head8[...] = jnp.zeros_like(head8)
        head8[: head_ref.shape[0]] = head_ref[...]

    for src, dst in ((q_ref, qo_ref), (k_ref, ko_ref), (v_ref, vo_ref)):
        dst[...] = src[...]
    a_high, a_low = split_bf16(a_ref[...])
    h_high, h_low = split_bf16(head8[...])
    out_ref[...] = mm(a_high, h_high, 0, 0) + (mm(a_high, h_low, 0, 0) + mm(a_low, h_high, 0, 0))


def per_device(sizes, query, key, value, stream, targets, short_filter, med_filter, out_weight, head):
    genomes, count, width = query.shape
    half = width // 2
    tiles = half // LANES
    rows = count + 2 * EDGE
    far = count - RIM
    own = out_weight.shape[0]
    taps = short_filter.shape[0]
    seqs, shards = sizes
    assert genomes == 1 and med_filter.shape == (PART, half // 16) and 4 < taps <= EDGE and count % 32 == 0 and ROWS < rows <= 2 * ROWS
    query, key, value, stream = (a.reshape(count, width) for a in (query, key, value, stream))

    sds = jax.ShapeDtypeStruct
    vmem = pl.BlockSpec(memory_space=pltpu.VMEM)
    hbm = pl.BlockSpec(memory_space=pl.ANY)
    dma = pltpu.SemaphoreType.DMA
    query_grad, key_grad, value_grad, a_sum = pl.pallas_call(
        functools.partial(block_kernel, sizes),
        in_specs=[hbm] * 4 + [vmem] * 3 + [hbm, vmem],
        out_specs=[hbm] * 3 + [vmem],
        out_shape=[sds((count, width), bf16)] * 3 + [sds((8, own), f32)],
        scratch_shapes=[
            pltpu.VMEM((count, width), bf16), pltpu.VMEM((count, width), bf16), pltpu.VMEM((count, width), bf16),
            pltpu.VMEM((count, width), bf16), pltpu.VMEM((own, half), bf16), pltpu.VMEM((3, count, width), bf16),
            pltpu.VMEM((4, RIM, width), bf16), pltpu.VMEM((2, RIM, width), bf16),
            pltpu.VMEM((RIM, half), bf16), pltpu.VMEM((RIM, half), bf16),
            pltpu.VMEM((RIM, width), bf16), pltpu.VMEM((RIM, width), bf16),
            pltpu.VMEM((2, 3, LANES // PART, count + 2 * RIM, PART), f32),
            pltpu.VMEM((2, rows, half), bf16), pltpu.VMEM((2, rows, half), bf16),
            pltpu.VMEM((PART, half), bf16), pltpu.VMEM((PART, half), bf16),
            pltpu.VMEM((far, half), bf16), pltpu.VMEM((far, half), bf16),
            pltpu.VMEM((2, rows, half), f32), pltpu.VMEM((2, rows, half), f32),
            pltpu.VMEM((2 * tiles, rows, LANES), f32),
            pltpu.VMEM((2, half // PART, 8 * ROWS, 2 * PART), bf16),
            pltpu.VMEM((2, count + far, LANES), bf16),
            pltpu.VMEM((2 * tiles, count, LANES), bf16),
            pltpu.VMEM((count, PART), f32), pltpu.VMEM((count, 16), f32),
            pltpu.VMEM((far, 16), f32), pltpu.VMEM((far, 16), f32),
            pltpu.VMEM((8, half), f32), pltpu.VMEM((shards, 8, own), f32), pltpu.VMEM((8, half), f32),
            pltpu.VMEM((2, 48, half), bf16), pltpu.VMEM((2, 32, half), bf16), pltpu.VMEM((2, count + far, 48), bf16),
            pltpu.VMEM((PART, LANES), f32),
            pltpu.VMEM((2, 1, rows, LANES), f32), pltpu.VMEM((2, 3, LANES // PART, rows, PART), f32),
            pltpu.VMEM((8, half), f32), pltpu.VMEM((shards, 8, own), f32), pltpu.VMEM((seqs, 8, own), f32),
            pltpu.VMEM((8, own), f32),
            dma((4,)), dma((5,)), dma((3, 2 * tiles)), dma((2, 2)), dma((2, 2)), dma((2, tiles)), dma((2, tiles)), dma((2, tiles)), dma((2, tiles)),
            dma((2,)), dma((2,)), dma((shards,)), dma((shards,)), dma((shards,)), dma((shards,)),
            dma((seqs,)), dma((seqs,)),
        ],
        compiler_params=pltpu.CompilerParams(collective_id=0, has_side_effects=True, vmem_limit_bytes=VMEM_LIMIT),
        cost_estimate=pl.CostEstimate(flops=1024 * count * width * 8, bytes_accessed=20 * count * width, transcendentals=0),
        name="hyena_block",
    )(query, key, value, stream, targets, short_filter.transpose(1, 0, 2), med_filter, out_weight, head)

    steps = own // 128
    piece = pl.BlockSpec((count, width // steps), lambda i: (0, i))
    query_grad, key_grad, value_grad, out_grad = pl.pallas_call(
        finish_kernel,
        grid=(steps,),
        in_specs=[pl.BlockSpec((8, 128), lambda i: (0, i)), pl.BlockSpec((NUC, half), lambda i: (0, 0))] + [piece] * 3,
        out_specs=[piece] * 3 + [pl.BlockSpec((128, half), lambda i: (i, 0))],
        out_shape=[sds((count, width), bf16)] * 3 + [sds((own, half), f32)],
        scratch_shapes=[pltpu.VMEM((8, half), f32)],
        compiler_params=pltpu.CompilerParams(vmem_limit_bytes=VMEM_LIMIT),
        name="finish",
    )(a_sum, head, query_grad, key_grad, value_grad)
    return (query_grad[None], key_grad[None], value_grad[None], out_grad)


def solution(mesh):
    rows = P("fsdp", "seq", None)
    return jax.shard_map(
        functools.partial(per_device, (mesh.shape["seq"], mesh.shape["fsdp"])),
        mesh=mesh,
        in_specs=(rows, rows, rows, rows, P("fsdp", "seq"), P(), P(), P("fsdp", None), P()),
        out_specs=(rows, rows, rows, P("fsdp", None)),
        check_vma=False,
    )
```
